32 devices in a mesh: groups: 2 (over y), expert: 4 (over z), width: 4 (over x, core).
Axes of the slice: x: 2, y: 2, z: 4, core: 2. Of those that a mesh axis runs over, the one named last changes fastest.
Arguments:
- residuals: bfloat16 [8192, 8192], P(('groups', 'expert'), 'width'), parts along dimension 0, may hold values from -6 to 6
- routes: int32 [8192, 1], P(('groups', 'expert')), parts along dimension 0, may hold values from 0 to 3; in each aligned block of 1024 rows (0 to 1023, 1024 to 2047, ...) at most 512 rows name the same one
- router_gate: bfloat16 [8192], P(('groups', 'expert')), parts along dimension 0, may hold values from 0.5 to 1
- enc_weight: bfloat16 [8, 8192, 256], P(('groups', 'expert'), 'width'), parts along dimension 0, may hold values from -0.0625 to 0.0625
- dec_weight: bfloat16 [8, 256, 8192], P(('groups', 'expert'), None, 'width'), parts along dimension 0, may hold values from -0.375 to 0.375
- enc_first: float32 [8, 8192, 256], P(('groups', 'expert'), 'width'), parts along dimension 0, may hold values from -3 to 3
- enc_second: float32 [8, 8192, 256], P(('groups', 'expert'), 'width'), parts along dimension 0, may hold values from 0.05 to 1
- dec_first: float32 [8, 256, 8192], P(('groups', 'expert'), None, 'width'), parts along dimension 0, may hold values from -3 to 3
- dec_second: float32 [8, 256, 8192], P(('groups', 'expert'), None, 'width'), parts along dimension 0, may hold values from 0.05 to 1
Outputs:
- new_enc_first: float32 [8, 8192, 256], P(('groups', 'expert'), 'width'), parts along dimension 0
- new_enc_second: float32 [8, 8192, 256], P(('groups', 'expert'), 'width'), parts along dimension 0
- enc_update: bfloat16 [8, 8192, 256], P(('groups', 'expert'), 'width'), parts along dimension 0
- new_dec_first: float32 [8, 256, 8192], P(('groups', 'expert'), None, 'width'), parts along dimension 0
- new_dec_second: float32 [8, 256, 8192], P(('groups', 'expert'), None, 'width'), parts along dimension 0
- dec_update: bfloat16 [8, 256, 8192], P(('groups', 'expert'), None, 'width'), parts along dimension 0
The draws below stay inside these ranges and needn't reach their ends.
There are 2 independent parts, one for each index of `groups`. The reference program is written for one: setup_inputs(seed, part) draws one part's arguments, and reference() takes and returns one part's arrays. A program takes and returns all parts, laid end to end along the dimension named above; each array names one. Nothing has to cross between parts.
Inputs may be any that keep to these rules, and one draw needn't show every extreme that they name: `routes`: each row names one expert. In each aligned block of 1024 rows no expert is named by more than 512 rows, a bound that some block reaches.
All inputs are finite; a program needn't handle non-finite values.
Results may differ from the reference program's by a relative error of at most 0.0039.
Values may be sent and summed in bfloat16 or wider, within the bound.
A program may use at most 128 MiB of HBM per device.

```python
import math
import jax
import jax.numpy as jnp
import numpy as np
from jax import lax

D = 8192
LAT = 256
ROW_DEV = 1024
STEP = 100
EXPERTS = 4
CAP = 512
ROWS = 4096


def block_scale(rng, shape, shards, smallest, high):
    gain, own = 1.0, jax.random.fold_in(rng, 6)
    for dim, shards_of in shards:
        draws = jnp.exp(jax.random.uniform(jax.random.fold_in(own, dim), (shards_of,), jnp.float32, smallest / len(shards), high / len(shards)))
        gain = gain * jnp.repeat(draws, shape[dim] // shards_of).reshape([-1 if axis == dim else 1 for axis in range(len(shape))])
    return gain


def assign_block(key, own, number, rows, amount, top, reach, lean):
    sequence = jax.random.permutation(key, amount)
    packed, common = portions_of(amount, rows * top, reach, lean, True), portions_of(amount, rows * top, reach, lean, False)
    places = jnp.arange(amount)

    def named(tallies, offset_by):
        used = int((tallies > 0).sum())
        fixed = max(1, used // 4)
        shifted = fixed + (places - fixed + offset_by * (used - fixed)) % max(1, amount - fixed)
        return jnp.zeros((amount,), jnp.int32).at[sequence[jnp.where(places < fixed, places, shifted)]].set(jnp.asarray(tallies, jnp.int32))

    tallies = jnp.where(number % 4 == 0, named(packed, number // 4), named(common, number - number // 4 - 1))
    mixed = jax.random.permutation(jax.random.fold_in(own, 3), amount)
    giver, sink = mixed[0:amount // 2 * 2:2], mixed[1:amount // 2 * 2:2]
    margin = jnp.minimum(tallies[giver] - 1, reach - tallies[sink]) // 2
    margin = jnp.where((giver == sequence[0]) | (sink == sequence[0]) | (tallies[sink] == 0), 0, jnp.maximum(margin, 0))
    shifted = jax.random.randint(jax.random.fold_in(own, 4), (amount // 2,), 0, 1 << 20) % (margin + 1)
    tallies = tallies.at[giver].add(-shifted).at[sink].add(shifted)
    items = jnp.searchsorted(jnp.cumsum(tallies), jnp.arange(rows * top), side="right").astype(jnp.int32)
    grid = items.reshape(top, rows).T
    grid = grid[jax.random.permutation(jax.random.fold_in(own, 1), rows)]
    offset_by = jax.random.randint(jax.random.fold_in(own, 2), (rows, 1), 0, top)
    return jnp.take_along_axis(grid, (jnp.arange(top)[None, :] + offset_by) % top, axis=1)


def portions_of(amount, total, reach, skew, full):
    portions = [(1 << 20) // math.isqrt(standing ** skew) + 1 for standing in range(1, amount + 1)]
    largest = reach if full else min(reach, max(-(-total // amount), total * portions[0] // sum(portions)))
    least = 1 if total - largest >= amount - 1 else 0
    given, rest = [largest] + [least] * (amount - 1), total - largest - least * (amount - 1)
    while rest > 0:
        free = [i for i in range(1, amount) if given[i] < largest] or [i for i in range(1, amount) if given[i] < reach]
        mass, remaining = sum([portions[i] for i in free]), rest
        for i in free:
            extra = min(reach - given[i], max(1, remaining * portions[i] // mass), rest)
            given[i] = given[i] + extra
            rest = rest - extra
    return np.array(given)


def normal_values(own_key, dims, deviation, bound, pieces=(), kind=jnp.bfloat16):
    level = block_scale(own_key, dims, pieces, -0.22, 0.18) if pieces else 1.0
    array = jax.random.normal(own_key, dims, jnp.float32) * deviation * level
    return jnp.minimum(jnp.maximum(array, -bound), bound).astype(kind)


def setup_inputs(seed: int = 0, part: int = 0) -> dict:
    seeds = jax.random.split(jax.random.key(seed), 10)
    own_keys = jax.random.split(jax.random.fold_in(seeds[9], part), 10)
    residuals = normal_values(own_keys[0], (ROWS, D), 1.0, 6.0, ((0, 4), (1, 4)))
    routes_keys = jax.random.split(jax.random.fold_in(own_keys[1], 1), ROWS // ROW_DEV)
    routes_turns = jax.random.permutation(jax.random.fold_in(own_keys[1], 3), ROWS // ROW_DEV)
    routes = jax.vmap(lambda own, number: assign_block(jax.random.fold_in(own_keys[1], 2), own, number, ROW_DEV, EXPERTS, 1, CAP, 2))(routes_keys, routes_turns).reshape((ROWS, 1))
    router_gate = jnp.clip(0.5 + 0.5 * jax.random.uniform(own_keys[2], (ROWS,), jnp.float32) ** block_scale(own_keys[2], (ROWS,), ((0, 4),), -0.2, 0.2), 0.5, 1.0).astype(jnp.bfloat16)
    enc_weight = normal_values(own_keys[3], (EXPERTS, D, LAT), D ** -0.5, 0.0625, ((0, 4), (1, 4)))
    dec_weight = normal_values(own_keys[4], (EXPERTS, LAT, D), LAT ** -0.5, 0.375, ((0, 4), (2, 4)))
    enc_first = normal_values(own_keys[5], (EXPERTS, D, LAT), 0.5, 3.0, ((0, 4), (1, 4)), jnp.float32)
    enc_second = jnp.clip(jnp.exp(math.log(1.0) - 2.9957323 * jax.random.uniform(own_keys[6], (EXPERTS, D, LAT), jnp.float32) ** block_scale(own_keys[6], (EXPERTS, D, LAT), ((0, 4), (1, 4)), -0.2, 0.2)), 0.05, 1.0)
    dec_first = normal_values(own_keys[7], (EXPERTS, LAT, D), 0.5, 3.0, ((0, 4), (2, 4)), jnp.float32)
    dec_second = jnp.clip(jnp.exp(math.log(1.0) - 2.9957323 * jax.random.uniform(own_keys[8], (EXPERTS, LAT, D), jnp.float32) ** block_scale(own_keys[8], (EXPERTS, LAT, D), ((0, 4), (2, 4)), -0.2, 0.2)), 0.05, 1.0)
    return {"residuals": residuals, "routes": routes, "router_gate": router_gate, "enc_weight": enc_weight, "dec_weight": dec_weight, "enc_first": enc_first, "enc_second": enc_second, "dec_first": dec_first, "dec_second": dec_second}


L1_COEF = 1.0
CLIP_RATIO = 0.5
BETA_ONE = 0.9
BETA_TWO = 0.999
ADAM_EPS = 1e-08

def expert_grads(slot_rows, slot_gate, w_enc, w_dec):
    preact = jnp.dot(slot_rows, w_enc, preferred_element_type=jnp.float32)
    codes = jnp.maximum(preact, 0.0).astype(jnp.bfloat16)
    decoded = jnp.dot(codes, w_dec, preferred_element_type=jnp.float32)
    errors = slot_gate[:, None] * decoded - slot_rows.astype(jnp.float32)
    grad_out = (2.0 * slot_gate[:, None] * errors).astype(jnp.bfloat16)
    grad_dec = jnp.dot(codes.T, grad_out, preferred_element_type=jnp.float32)
    grad_codes = jnp.dot(grad_out, w_dec.T, preferred_element_type=jnp.float32)
    grad_pre = jnp.where(codes > 0, grad_codes + L1_COEF, 0.0).astype(jnp.bfloat16)
    grad_enc = jnp.dot(slot_rows.T, grad_pre, preferred_element_type=jnp.float32)
    return (grad_enc, grad_dec)

def adam_step(first, second, gradient, factor):
    scaled = factor * gradient
    new_first = BETA_ONE * first + (1.0 - BETA_ONE) * scaled
    new_second = BETA_TWO * second + (1.0 - BETA_TWO) * scaled * scaled
    corrected = new_first / (1.0 - BETA_ONE ** STEP)
    spread = jnp.sqrt(new_second / (1.0 - BETA_TWO ** STEP))
    return (new_first, new_second, (corrected / (spread + ADAM_EPS)).astype(jnp.bfloat16))

def reference(residuals, routes, router_gate, enc_weight, dec_weight, enc_first, enc_second, dec_first, dec_second):
    slots = 2 * ROW_DEV
    flat_route = routes[:, 0]
    order = jnp.argsort(flat_route, stable=True).astype(jnp.int32)
    expert_ids = jnp.arange(EXPERTS, dtype=jnp.int32)
    counts = lax.optimization_barrier(jnp.sum((flat_route[:, None] == expert_ids[None, :]).astype(jnp.int32), axis=0))
    offsets = (jnp.cumsum(counts) - counts).astype(jnp.int32)
    sorted_rows = jnp.concatenate([residuals[order], jnp.zeros((slots, D), jnp.bfloat16)], axis=0)
    sorted_gate = jnp.concatenate([router_gate[order].astype(jnp.float32), jnp.zeros((slots,), jnp.float32)], axis=0)
    positions = jnp.arange(slots, dtype=jnp.int32)

    def one_expert(expert):
        start = offsets[expert].astype(jnp.int32)
        rows = lax.dynamic_slice_in_dim(sorted_rows, start, slots, 0)
        gates = lax.dynamic_slice_in_dim(sorted_gate, start, slots, 0)
        live = positions < counts[expert]
        rows = jnp.where(live[:, None], rows, jnp.zeros_like(rows))
        gates = jnp.where(live, gates, jnp.zeros_like(gates))
        return expert_grads(rows, gates, enc_weight[expert], dec_weight[expert])
    grad_enc, grad_dec = lax.map(one_expert, expert_ids)
    total = jnp.sum(grad_enc * grad_enc) + jnp.sum(grad_dec * grad_dec)
    limit = CLIP_RATIO * math.sqrt(2.0 * EXPERTS * D * LAT)
    factor = jnp.minimum(1.0, limit / (jnp.sqrt(total) + 1e-06))
    enc_new_first, enc_new_second, enc_direction = adam_step(enc_first, enc_second, grad_enc, factor)
    dec_new_first, dec_new_second, dec_direction = adam_step(dec_first, dec_second, grad_dec, factor)
    return (enc_new_first, enc_new_second, enc_direction, dec_new_first, dec_new_second, dec_direction)
```

```python
import functools
import math

import jax
import jax.numpy as jnp
from jax import lax
from jax.experimental import pallas as pl
from jax.experimental.pallas import tpu as pltpu
from jax.sharding import PartitionSpec as P

STEP = 100
L1_COEF = 1.0
CLIP_RATIO = 0.5
BETA_ONE = 0.9
BETA_TWO = 0.999
ADAM_EPS = 1e-08
MESH = pl.DeviceIdType.MESH
BF, F32 = jnp.bfloat16, jnp.float32


def dot(a, b, ca=1, cb=0):
    return lax.dot_general(a, b, (((ca,), (cb,)), ((), ())), preferred_element_type=F32)


def adam_step(first, second, gradient, factor):
    scaled = factor * gradient
    new_first = BETA_ONE * first + (1.0 - BETA_ONE) * scaled
    new_second = BETA_TWO * second + (1.0 - BETA_TWO) * scaled * scaled
    corrected = new_first / (1.0 - BETA_ONE**STEP)
    spread = jnp.sqrt(new_second / (1.0 - BETA_TWO**STEP))
    return (new_first, new_second, (corrected / (spread + ADAM_EPS)).astype(BF))


def kernel(
    experts, widths, cap, chunk, tile,
    x_ref, route_ref, gate_ref, we_ref, wd_ref,
    ge_ref, gd_ref, tot_ref,
    snd, rows, gsnd, grow, pre, pre_in, codes, gc, gc_in, gp, acc, gout, norm,
    z_send, z_recv, g_send, g_recv, p_send, p_recv, c_send, c_recv,
    b_send, b_recv, q_send, q_recv, n_send, n_recv,
):
    local_rows, feats = x_ref.shape
    halves = cap // chunk
    count = experts * halves
    quarter = chunk // widths
    me = lax.axis_index("expert")
    mw = lax.axis_index("width")

    def zdev(d):
        return {"expert": lax.rem(me + d, experts)}

    def wdev(w):
        return {"width": lax.rem(mw + w, widths)}

    barrier = pltpu.get_barrier_semaphore()
    for d in range(1, experts):
        pl.semaphore_signal(barrier, inc=1, device_id=zdev(d), device_id_type=MESH)
    for w in range(1, widths):
        pl.semaphore_signal(barrier, inc=1, device_id=wdev(w), device_id_type=MESH)

    pad = max(16, experts)
    route = route_ref[...]
    named = (lax.broadcasted_iota(jnp.int32, (pad, local_rows), 0) == route).astype(BF)
    upper = (
        lax.broadcasted_iota(jnp.int32, (local_rows, local_rows), 0)
        <= lax.broadcasted_iota(jnp.int32, (local_rows, local_rows), 1)
    ).astype(BF)
    within = jnp.sum(dot(named, upper) * named.astype(F32), axis=0, keepdims=True)
    target = route * cap + within.astype(jnp.int32) - 1
    pl.semaphore_wait(barrier, experts + widths - 2)

    half_way = experts // 2
    order = [0] + sorted(range(1, experts), key=lambda d: (abs(d - half_way), d))

    def z_copy(n, d):
        m = n - halves
        return pltpu.make_async_remote_copy(
            snd.at[m], rows.at[n], z_send.at[m], z_recv.at[m], device_id=zdev(d), device_id_type=MESH
        )

    def g_copy(n, d):
        m = n - halves
        return pltpu.make_async_remote_copy(
            gsnd.at[m], grow.at[n], g_send.at[m], g_recv.at[m], device_id=zdev(d), device_id_type=MESH
        )

    for j in [*range(1, experts), 0]:
        expert = lax.rem(me + order[j], experts)
        for h in range(halves):
            n = j * halves + h
            base = expert * cap + h * chunk
            slot = lax.broadcasted_iota(jnp.int32, (chunk, local_rows), 0) + base
            pick = (slot == target).astype(BF)
            to, gto = (snd.at[n - halves], gsnd.at[n - halves]) if j else (rows.at[n], grow.at[n])
            gto[...] = dot(gate_ref[...], pick, 1, 1).astype(BF)

            @pl.loop(0, feats // tile)
            def _(f):
                cols = pl.ds(pl.multiple_of(f * tile, tile), tile)
                to[:, cols] = dot(pick, x_ref[:, cols]).astype(BF)

            if j:
                g_copy(n, order[j]).start()
                z_copy(n, order[j]).start()

    ge_ref[...] = jnp.zeros_like(ge_ref)
    gd_ref[...] = jnp.zeros_like(gd_ref)
    mine = pl.ds(pl.multiple_of(mw * quarter, quarter), quarter)

    def scatter(n, w, src, dst, ssem, rsem):
        theirs = lax.rem(mw + w, widths)
        return pltpu.make_async_remote_copy(
            src.at[n, pl.ds(pl.multiple_of(theirs * quarter, quarter), quarter)],
            dst.at[n, w - 1],
            ssem.at[n, w - 1], rsem.at[n, w - 1], device_id=wdev(w), device_id_type=MESH,
        )

    def gather(n, w, buf, ssem, rsem):
        return pltpu.make_async_remote_copy(
            buf.at[n, mine], buf.at[n, mine],
            ssem.at[n, w - 1], rsem.at[n, w - 1], device_id=wdev(w), device_id_type=MESH,
        )

    def gather_wait(n, w, buf, ssem, rsem):
        src = lax.rem(mw + widths - w, widths)
        theirs = pl.ds(pl.multiple_of(src * quarter, quarter), quarter)
        pltpu.make_async_remote_copy(
            buf.at[n, theirs], buf.at[n, theirs],
            ssem.at[n, w - 1], rsem.at[n, w - 1], device_id=wdev(w), device_id_type=MESH,
        ).wait_recv()

    peers = range(1, widths)

    def stage_pre(n):
        @pl.when(n >= halves)
        def _():
            z_copy(n, 1).wait_recv()
            g_copy(n, 1).wait_recv()

        pre[n] = dot(rows[n], we_ref[...])
        for w in peers:
            scatter(n, w, pre, pre_in, p_send, p_recv).start()

    def stage_codes(n):
        total = pre[n, mine]
        for w in peers:
            scatter(n, w, pre, pre_in, p_send, p_recv).wait_recv()
            total = total + pre_in[n, w - 1]
        codes[n, mine] = jnp.maximum(total, 0.0).astype(BF)
        for w in peers:
            gather(n, w, codes, c_send, c_recv).start()

    def stage_decode(n):
        for w in peers:
            gather_wait(n, w, codes, c_send, c_recv)
        gate = grow[n].astype(F32).T[:, :1]
        code = codes[n]
        acc[...] = jnp.zeros_like(acc)

        @pl.loop(0, feats // tile)
        def _(f):
            cols = pl.ds(pl.multiple_of(f * tile, tile), tile)
            w_dec = wd_ref[:, cols]
            errors = gate * dot(code, w_dec) - rows[n, :, cols].astype(F32)
            gout[:, cols] = (2.0 * gate * errors).astype(BF)
            go = gout[:, cols]
            acc[...] += dot(go, w_dec, 1, 1)
            gd_ref[:, cols] += dot(code, go, 0, 0)

        gc[n] = acc[...].astype(BF)
        for w in peers:
            scatter(n, w, gc, gc_in, b_send, b_recv).start()

    def stage_gradpre(n):
        total = gc[n, mine].astype(F32)
        for w in peers:
            scatter(n, w, gc, gc_in, b_send, b_recv).wait_recv()
            total = total + gc_in[n, w - 1].astype(F32)
        gp[n, mine] = jnp.where(codes[n, mine].astype(F32) > 0, total + L1_COEF, 0.0).astype(BF)
        for w in peers:
            gather(n, w, gp, q_send, q_recv).start()

    def stage_encgrad(n):
        for w in peers:
            gather_wait(n, w, gp, q_send, q_recv)
        grad_pre = gp[n]

        @pl.loop(0, feats // tile)
        def _(f):
            cols = pl.ds(pl.multiple_of(f * tile, tile), tile)
            ge_ref[cols, :] += dot(rows[n, :, cols], grad_pre, 0, 0)

    stages = (stage_pre, stage_codes, stage_decode, stage_gradpre, stage_encgrad)

    @pl.loop(0, count + len(stages) - 1)
    def _(t):
        for lag in reversed(range(len(stages))):
            @pl.when((t >= lag) & (t < count + lag))
            def _(lag=lag):
                stages[lag](t - lag)

    square = jnp.sum(ge_ref[...] * ge_ref[...]) + jnp.sum(gd_ref[...] * gd_ref[...])
    norm[0] = jnp.full(norm.shape[1:], square, F32)
    first = [
        pltpu.make_async_remote_copy(
            norm.at[0], norm.at[1 + w], n_send.at[w], n_recv.at[w], device_id=wdev(w), device_id_type=MESH
        )
        for w in peers
    ]
    for c in first:
        c.start()
    for c in first:
        c.wait()
    part = norm[0]
    for w in peers:
        part = part + norm[1 + w]
    norm[1] = part
    off = widths + 1
    second = [
        pltpu.make_async_remote_copy(
            norm.at[1], norm.at[off + d], n_send.at[widths + d], n_recv.at[widths + d],
            device_id=zdev(d), device_id_type=MESH,
        )
        for d in range(1, experts)
    ]
    for c in second:
        c.start()
    for c in second:
        c.wait()
    for d in range(1, experts):
        part = part + norm[off + d]
    tot_ref[...] = part

    @pl.loop(halves, count)
    def _(n):
        z_copy(n, 1).wait_send()
        g_copy(n, 1).wait_send()

    @pl.loop(0, count)
    def _(n):
        for w in peers:
            scatter(n, w, pre, pre_in, p_send, p_recv).wait_send()
            gather(n, w, codes, c_send, c_recv).wait_send()
            scatter(n, w, gc, gc_in, b_send, b_recv).wait_send()
            gather(n, w, gp, q_send, q_recv).wait_send()


def body(
    residuals, routes, router_gate, enc_weight, dec_weight, enc_first, enc_second, dec_first, dec_second
):
    experts = lax.axis_size("expert")
    widths = lax.axis_size("width")
    local_rows, feats = residuals.shape
    lat = enc_weight.shape[2]
    cap = 2 * local_rows // experts
    chunk = min(256, cap)
    tile = min(512, feats)
    halves = cap // chunk
    count = experts * halves
    quarter = chunk // widths
    far = count - halves
    route = routes.reshape(1, local_rows)
    gate = jnp.broadcast_to(router_gate[None, :], (16, local_rows))
    vmem = pl.BlockSpec(memory_space=pltpu.VMEM)
    dma = pltpu.SemaphoreType.DMA
    grad_enc, grad_dec, total = pl.pallas_call(
        functools.partial(kernel, experts, widths, cap, chunk, tile),
        out_shape=(
            jax.ShapeDtypeStruct((feats, lat), F32),
            jax.ShapeDtypeStruct((lat, feats), F32),
            jax.ShapeDtypeStruct((8, 128), F32),
        ),
        in_specs=[vmem] * 5,
        out_specs=(vmem,) * 3,
        scratch_shapes=[
            pltpu.VMEM((far, chunk, feats), BF),
            pltpu.VMEM((count, chunk, feats), BF),
            pltpu.VMEM((far, 16, chunk), BF),
            pltpu.VMEM((count, 16, chunk), BF),
            pltpu.VMEM((count, chunk, lat), F32),
            pltpu.VMEM((count, widths - 1, quarter, lat), F32),
            pltpu.VMEM((count, chunk, lat), BF),
            pltpu.VMEM((count, chunk, lat), BF),
            pltpu.VMEM((count, widths - 1, quarter, lat), BF),
            pltpu.VMEM((count, chunk, lat), BF),
            pltpu.VMEM((chunk, lat), F32),
            pltpu.VMEM((chunk, feats), BF),
            pltpu.VMEM((1 + widths + experts, 8, 128), F32),
            dma((far,)), dma((far,)), dma((far,)), dma((far,)),
            *[dma((count, widths - 1)) for _ in range(8)],
            dma((widths + experts,)), dma((widths + experts,)),
        ],
        compiler_params=pltpu.CompilerParams(
            collective_id=0, has_side_effects=True, vmem_limit_bytes=56 * 1024 * 1024
        ),
        cost_estimate=pl.CostEstimate(
            flops=10 * count * chunk * feats * lat, bytes_accessed=16 * feats * lat, transcendentals=0
        ),
    )(residuals, route, gate, enc_weight[0], dec_weight[0])
    param_count = 2.0 * experts * enc_weight.shape[0] * feats * widths * lat
    norm = jnp.sqrt(total[0, 0])
    factor = jnp.minimum(1.0, CLIP_RATIO * math.sqrt(param_count) / (norm + 1e-06))
    return (
        *adam_step(enc_first, enc_second, grad_enc[None], factor),
        *adam_step(dec_first, dec_second, grad_dec[None], factor),
    )


def solution(mesh):
    row = P(("groups", "expert"), "width")
    enc = P(("groups", "expert"), "width", None)
    dec = P(("groups", "expert"), None, "width")
    in_specs = (row, P(("groups", "expert"), None), P(("groups", "expert")), enc, dec, enc, enc, dec, dec)
    out_specs = (enc, enc, enc, dec, dec, dec)
    return jax.shard_map(body, mesh=mesh, in_specs=in_specs, out_specs=out_specs, check_vma=False)
```

```python
import functools
import math

import jax
import jax.numpy as jnp
from jax import lax
from jax.experimental import pallas as pl
from jax.experimental.pallas import tpu as pltpu
from jax.sharding import PartitionSpec as P

STEP = 100
L1_COEF = 1.0
CLIP_RATIO = 0.5
BETA_ONE = 0.9
BETA_TWO = 0.999
ADAM_EPS = 1e-08
MESH = pl.DeviceIdType.MESH
BF, F32 = jnp.bfloat16, jnp.float32


def dot(a, b, ca=1, cb=0):
    return lax.dot_general(a, b, (((ca,), (cb,)), ((), ())), preferred_element_type=F32)


def adam_step(first, second, gradient, factor):
    scaled = factor * gradient
    new_first = BETA_ONE * first + (1.0 - BETA_ONE) * scaled
    new_second = BETA_TWO * second + (1.0 - BETA_TWO) * scaled * scaled
    corrected = new_first / (1.0 - BETA_ONE**STEP)
    spread = jnp.sqrt(new_second / (1.0 - BETA_TWO**STEP))
    return (new_first, new_second, (corrected / (spread + ADAM_EPS)).astype(BF))


def kernel(
    experts, widths, cap, chunk, tile,
    x_ref, route_ref, gate_ref, we_ref, wd_ref,
    ge_ref, gd_ref, tot_ref,
    snd, rows, gsnd, grow, pre, pre_in, codes, gc, gc_in, gp, acc, gout, norm,
    z_send, z_recv, g_send, g_recv, p_send, p_recv, c_send, c_recv,
    b_send, b_recv, q_send, q_recv, n_send, n_recv,
):
    local_rows, feats = x_ref.shape
    halves = cap // chunk
    count = experts * halves
    quarter = chunk // widths
    me = lax.axis_index("expert")
    mw = lax.axis_index("width")

    def zdev(d):
        return {"expert": lax.rem(me + d, experts)}

    def wdev(w):
        return {"width": lax.rem(mw + w, widths)}

    barrier = pltpu.get_barrier_semaphore()
    for d in range(1, experts):
        pl.semaphore_signal(barrier, inc=1, device_id=zdev(d), device_id_type=MESH)
    for w in range(1, widths):
        pl.semaphore_signal(barrier, inc=1, device_id=wdev(w), device_id_type=MESH)

    pad = max(16, experts)
    route = route_ref[...]
    named = (lax.broadcasted_iota(jnp.int32, (pad, local_rows), 0) == route).astype(BF)
    upper = (
        lax.broadcasted_iota(jnp.int32, (local_rows, local_rows), 0)
        <= lax.broadcasted_iota(jnp.int32, (local_rows, local_rows), 1)
    ).astype(BF)
    within = jnp.sum(dot(named, upper) * named.astype(F32), axis=0, keepdims=True)
    target = route * cap + within.astype(jnp.int32) - 1
    pl.semaphore_wait(barrier, experts + widths - 2)

    depth = 3
    half_way = experts // 2
    order = [0] + sorted(range(1, experts), key=lambda d: (abs(d - half_way), d))

    def z_copy(n, d):
        m = n - halves
        return pltpu.make_async_remote_copy(
            snd.at[m], rows.at[n], z_send.at[m], z_recv.at[m], device_id=zdev(d), device_id_type=MESH
        )

    def g_copy(n, d):
        m = n - halves
        return pltpu.make_async_remote_copy(
            gsnd.at[m], grow.at[n], g_send.at[m], g_recv.at[m], device_id=zdev(d), device_id_type=MESH
        )

    for j in [*range(1, experts), 0]:
        expert = lax.rem(me + order[j], experts)
        for h in range(halves):
            n = j * halves + h
            base = expert * cap + h * chunk
            slot = lax.broadcasted_iota(jnp.int32, (chunk, local_rows), 0) + base
            pick = (slot == target).astype(BF)
            to, gto = (snd.at[n - halves], gsnd.at[n - halves]) if j else (rows.at[n], grow.at[n])
            gto[...] = dot(gate_ref[...], pick, 1, 1).astype(BF)

            @pl.loop(0, feats // tile)
            def _(f):
                cols = pl.ds(pl.multiple_of(f * tile, tile), tile)
                to[:, cols] = dot(pick, x_ref[:, cols]).astype(BF)

            if j:
                g_copy(n, order[j]).start()
                if n < halves + depth:
                    z_copy(n, order[j]).start()

    ge_ref[...] = jnp.zeros_like(ge_ref)
    gd_ref[...] = jnp.zeros_like(gd_ref)
    mine = pl.ds(pl.multiple_of(mw * quarter, quarter), quarter)

    def scatter(n, w, src, dst, ssem, rsem):
        theirs = lax.rem(mw + w, widths)
        return pltpu.make_async_remote_copy(
            src.at[n, pl.ds(pl.multiple_of(theirs * quarter, quarter), quarter)],
            dst.at[n, w - 1],
            ssem.at[n, w - 1], rsem.at[n, w - 1], device_id=wdev(w), device_id_type=MESH,
        )

    def gather(n, w, buf, ssem, rsem):
        return pltpu.make_async_remote_copy(
            buf.at[n, mine], buf.at[n, mine],
            ssem.at[n, w - 1], rsem.at[n, w - 1], device_id=wdev(w), device_id_type=MESH,
        )

    def gather_wait(n, w, buf, ssem, rsem):
        src = lax.rem(mw + widths - w, widths)
        theirs = pl.ds(pl.multiple_of(src * quarter, quarter), quarter)
        pltpu.make_async_remote_copy(
            buf.at[n, theirs], buf.at[n, theirs],
            ssem.at[n, w - 1], rsem.at[n, w - 1], device_id=wdev(w), device_id_type=MESH,
        ).wait_recv()

    peers = range(1, widths)

    def stage_pre(n):
        @pl.when(n >= halves)
        def _():
            z_copy(n, 1).wait_recv()
            g_copy(n, 1).wait_recv()
            z_copy(n, 1).wait_send()

        for j in range(1, experts):
            later = n + depth
            begin = max(j * halves, halves + depth)

            @pl.when((n >= halves) & (later >= begin) & (later < (j + 1) * halves))
            def _(j=j, later=later):
                z_copy(later, order[j]).start()

        pre[n] = dot(rows[n], we_ref[...])
        for w in peers:
            scatter(n, w, pre, pre_in, p_send, p_recv).start()

    def stage_codes(n):
        total = pre[n, mine]
        for w in peers:
            scatter(n, w, pre, pre_in, p_send, p_recv).wait_recv()
            total = total + pre_in[n, w - 1]
        codes[n, mine] = jnp.maximum(total, 0.0).astype(BF)
        for w in peers:
            gather(n, w, codes, c_send, c_recv).start()

    def stage_decode(n):
        for w in peers:
            gather_wait(n, w, codes, c_send, c_recv)
        gate = grow[n].astype(F32).T[:, :1]
        code = codes[n]
        acc[...] = jnp.zeros_like(acc)

        @pl.loop(0, feats // tile)
        def _(f):
            cols = pl.ds(pl.multiple_of(f * tile, tile), tile)
            w_dec = wd_ref[:, cols]
            errors = gate * dot(code, w_dec) - rows[n, :, cols].astype(F32)
            gout[:, cols] = (2.0 * gate * errors).astype(BF)
            go = gout[:, cols]
            acc[...] += dot(go, w_dec, 1, 1)
            gd_ref[:, cols] += dot(code, go, 0, 0)

        gc[n] = acc[...].astype(BF)
        for w in peers:
            scatter(n, w, gc, gc_in, b_send, b_recv).start()

    def stage_gradpre(n):
        total = gc[n, mine].astype(F32)
        for w in peers:
            scatter(n, w, gc, gc_in, b_send, b_recv).wait_recv()
            total = total + gc_in[n, w - 1].astype(F32)
        gp[n, mine] = jnp.where(codes[n, mine].astype(F32) > 0, total + L1_COEF, 0.0).astype(BF)
        for w in peers:
            gather(n, w, gp, q_send, q_recv).start()

    def stage_encgrad(n):
        for w in peers:
            gather_wait(n, w, gp, q_send, q_recv)
        grad_pre = gp[n]

        @pl.loop(0, feats // tile)
        def _(f):
            cols = pl.ds(pl.multiple_of(f * tile, tile), tile)
            ge_ref[cols, :] += dot(rows[n, :, cols], grad_pre, 0, 0)

    stages = (stage_pre, stage_codes, stage_decode, stage_gradpre, stage_encgrad)

    @pl.loop(0, count + len(stages) - 1)
    def _(t):
        for lag in reversed(range(len(stages))):
            @pl.when((t >= lag) & (t < count + lag))
            def _(lag=lag):
                stages[lag](t - lag)

    square = jnp.sum(ge_ref[...] * ge_ref[...]) + jnp.sum(gd_ref[...] * gd_ref[...])
    norm[0] = jnp.full(norm.shape[1:], square, F32)
    first = [
        pltpu.make_async_remote_copy(
            norm.at[0], norm.at[1 + w], n_send.at[w], n_recv.at[w], device_id=wdev(w), device_id_type=MESH
        )
        for w in peers
    ]
    for c in first:
        c.start()
    for c in first:
        c.wait()
    part = norm[0]
    for w in peers:
        part = part + norm[1 + w]
    norm[1] = part
    off = widths + 1
    second = [
        pltpu.make_async_remote_copy(
            norm.at[1], norm.at[off + d], n_send.at[widths + d], n_recv.at[widths + d],
            device_id=zdev(d), device_id_type=MESH,
        )
        for d in range(1, experts)
    ]
    for c in second:
        c.start()
    for c in second:
        c.wait()
    for d in range(1, experts):
        part = part + norm[off + d]
    tot_ref[...] = part

    @pl.loop(halves, count)
    def _(n):
        g_copy(n, 1).wait_send()

    @pl.loop(0, count)
    def _(n):
        for w in peers:
            scatter(n, w, pre, pre_in, p_send, p_recv).wait_send()
            gather(n, w, codes, c_send, c_recv).wait_send()
            scatter(n, w, gc, gc_in, b_send, b_recv).wait_send()
            gather(n, w, gp, q_send, q_recv).wait_send()


def body(
    residuals, routes, router_gate, enc_weight, dec_weight, enc_first, enc_second, dec_first, dec_second
):
    experts = lax.axis_size("expert")
    widths = lax.axis_size("width")
    local_rows, feats = residuals.shape
    lat = enc_weight.shape[2]
    cap = 2 * local_rows // experts
    chunk = min(256, cap)
    tile = min(512, feats)
    halves = cap // chunk
    count = experts * halves
    quarter = chunk // widths
    far = count - halves
    route = routes.reshape(1, local_rows)
    gate = jnp.broadcast_to(router_gate[None, :], (16, local_rows))
    vmem = pl.BlockSpec(memory_space=pltpu.VMEM)
    dma = pltpu.SemaphoreType.DMA
    grad_enc, grad_dec, total = pl.pallas_call(
        functools.partial(kernel, experts, widths, cap, chunk, tile),
        out_shape=(
            jax.ShapeDtypeStruct((feats, lat), F32),
            jax.ShapeDtypeStruct((lat, feats), F32),
            jax.ShapeDtypeStruct((8, 128), F32),
        ),
        in_specs=[vmem] * 5,
        out_specs=(vmem,) * 3,
        scratch_shapes=[
            pltpu.VMEM((far, chunk, feats), BF),
            pltpu.VMEM((count, chunk, feats), BF),
            pltpu.VMEM((far, 16, chunk), BF),
            pltpu.VMEM((count, 16, chunk), BF),
            pltpu.VMEM((count, chunk, lat), F32),
            pltpu.VMEM((count, widths - 1, quarter, lat), F32),
            pltpu.VMEM((count, chunk, lat), BF),
            pltpu.VMEM((count, chunk, lat), BF),
            pltpu.VMEM((count, widths - 1, quarter, lat), BF),
            pltpu.VMEM((count, chunk, lat), BF),
            pltpu.VMEM((chunk, lat), F32),
            pltpu.VMEM((chunk, feats), BF),
            pltpu.VMEM((1 + widths + experts, 8, 128), F32),
            dma((far,)), dma((far,)), dma((far,)), dma((far,)),
            *[dma((count, widths - 1)) for _ in range(8)],
            dma((widths + experts,)), dma((widths + experts,)),
        ],
        compiler_params=pltpu.CompilerParams(
            collective_id=0, has_side_effects=True, vmem_limit_bytes=56 * 1024 * 1024
        ),
        cost_estimate=pl.CostEstimate(
            flops=10 * count * chunk * feats * lat, bytes_accessed=16 * feats * lat, transcendentals=0
        ),
    )(residuals, route, gate, enc_weight[0], dec_weight[0])
    param_count = 2.0 * experts * enc_weight.shape[0] * feats * widths * lat
    norm = jnp.sqrt(total[0, 0])
    factor = jnp.minimum(1.0, CLIP_RATIO * math.sqrt(param_count) / (norm + 1e-06))
    return (
        *adam_step(enc_first, enc_second, grad_enc[None], factor),
        *adam_step(dec_first, dec_second, grad_dec[None], factor),
    )


def solution(mesh):
    row = P(("groups", "expert"), "width")
    enc = P(("groups", "expert"), "width", None)
    dec = P(("groups", "expert"), None, "width")
    in_specs = (row, P(("groups", "expert"), None), P(("groups", "expert")), enc, dec, enc, enc, dec, dec)
    out_specs = (enc, enc, enc, dec, dec, dec)
    return jax.shard_map(body, mesh=mesh, in_specs=in_specs, out_specs=out_specs, check_vma=False)
```
